128 devices in a mesh: row: 8 (over z, core), col: 16 (over y, x).
Axes of the slice: x: 4, y: 4, z: 4, core: 2. Of those that a mesh axis runs over, the one named last changes fastest.
Arguments:
- orbitals: bfloat16 [262144, 1920], P(('row', 'col')), may hold values from -6 to 6
- point_cell: int32 [8, 16, 128], P('row', 'col'), may hold values from 0 to 262143, as said below
- point_count: int32 [8, 16], P('row', 'col'), may hold values from 64 to 128, as said below
- kernel: bfloat16 [8, 16, 128, 8, 16, 128], P('row', None, None, None, 'col'), may hold values from -0.0009765625 to 0.0009765625
Outputs:
- exchange_points: float32 [8, 16, 128, 1920], P('row', 'col')
The draws below stay inside these ranges and needn't reach their ends.
Inputs may be any that keep to these rules, and one draw needn't show every extreme that they name: `point_cell`: the slots of block (r, c) name distinct cells of slab 16 r + c, that is of [(16 r + c) * 2048, (16 r + c + 1) * 2048); slots at or past the block's count are drawn the same way and not used. `point_count`: some block holds 128 live points in every draw.
All inputs are finite; a program needn't handle non-finite values.
Results may differ from the reference program's by a relative error of at most 0.0029.
Values may be sent and summed in bfloat16 or wider, within the bound.
No kernel may reach another device: no remote copies, remote signals or barrier semaphores. Data moves between devices by JAX's collectives and lax.ppermute only.
A program may use at most 128 MiB of HBM per device.

```python
import jax
import jax.numpy as jnp
from jax import lax

ORBITAL_COUNT = 1920
SLAB_SLOT_LIMIT = 128
GRID_DEV = 2048
NGRID = 262144
TOTAL_SLOTS = 16384
N_ROW = 8
N_COL = 16


def draw_point_count(key, part):
    key = jax.random.fold_in(key, 11)
    first, second = jax.random.split(key)
    slabs = N_ROW * N_COL
    counts = jax.random.randint(first, (slabs,), SLAB_SLOT_LIMIT // 2, SLAB_SLOT_LIMIT + 1)
    complete_slab = jax.random.randint(second, (), 0, slabs)
    counts = jnp.where(jnp.arange(slabs) == complete_slab, SLAB_SLOT_LIMIT, counts)
    return counts.reshape(N_ROW, N_COL).astype(jnp.int32)


def draw_point_cell(key, part):
    key = jax.random.fold_in(key, 23)
    slabs = N_ROW * N_COL
    scores = jax.random.randint(key, (slabs, GRID_DEV), 0, 1 << 16) * GRID_DEV
    scores = scores + jnp.arange(GRID_DEV, dtype=jnp.int32)[None, :]
    order = jnp.argsort(scores, axis=1)[:, :SLAB_SLOT_LIMIT].astype(jnp.int32)
    cells = order + (jnp.arange(slabs, dtype=jnp.int32) * GRID_DEV)[:, None]
    return cells.reshape(N_ROW, N_COL, SLAB_SLOT_LIMIT).astype(jnp.int32)


def block_levels(stream_key, shape, cuts, least, largest):
    factor_of, own = 1.0, jax.random.fold_in(stream_key, 6)
    for dim, blocks in cuts:
        steps = jnp.exp(jax.random.uniform(jax.random.fold_in(own, dim), (blocks,), jnp.float32, least / len(cuts), largest / len(cuts)))
        factor_of = factor_of * jnp.repeat(steps, shape[dim] // blocks).reshape([-1 if axis == dim else 1 for axis in range(len(shape))])
    return factor_of


def centred(own_key, extent, scale, bound, pieces=(), held_as=jnp.bfloat16):
    factor_of = block_levels(own_key, extent, pieces, -0.22, 0.18) if pieces else 1.0
    array = jax.random.normal(own_key, extent, jnp.float32) * scale * factor_of
    return jnp.minimum(jnp.maximum(array, -bound), bound).astype(held_as)


def setup_inputs(seed: int = 0) -> dict:
    streams_of = jax.random.split(jax.random.key(seed), 5)
    return {
        "orbitals": centred(streams_of[0], (NGRID, ORBITAL_COUNT), 1.0, 6.0, ((0, 128),)),
        "point_cell": draw_point_cell(jax.random.fold_in(streams_of[4], 71), 0),
        "point_count": draw_point_count(jax.random.fold_in(streams_of[4], 71), 0),
        "kernel": centred(streams_of[3], (N_ROW, N_COL, SLAB_SLOT_LIMIT, N_ROW, N_COL, SLAB_SLOT_LIMIT), (ORBITAL_COUNT * TOTAL_SLOTS) ** -0.5, 0.0009765625, ((0, 8), (4, 16))),
    }


def reference(orbitals, point_cell, point_count, kernel):
    orbital_count = orbitals.shape[1]
    live = jnp.arange(SLAB_SLOT_LIMIT, dtype=jnp.int32)[None, None, :] < point_count[:, :, None]
    orbital_values = jnp.where(live[:, :, :, None], orbitals[point_cell], jnp.zeros((), orbitals.dtype))
    orbital_values = orbital_values.astype(jnp.bfloat16).reshape(TOTAL_SLOTS, orbital_count)
    weight_factors = kernel.reshape(TOTAL_SLOTS, TOTAL_SLOTS)
    block = N_COL * SLAB_SLOT_LIMIT

    def one_block(start):
        rows = lax.dynamic_slice_in_dim(orbital_values, start, block, 0)
        gram = lax.dot_general(rows, orbital_values, (((1,), (1,)), ((), ())), preferred_element_type=jnp.float32)
        kern = lax.dynamic_slice_in_dim(weight_factors, start, block, 0).astype(jnp.float32)
        weighted = (gram * kern).astype(jnp.bfloat16)
        return jnp.dot(weighted, orbital_values, preferred_element_type=jnp.float32)

    starts = (jnp.arange(N_ROW, dtype=jnp.int32) * block).astype(jnp.int32)
    result = lax.map(one_block, starts)
    return result.reshape(N_ROW, N_COL, SLAB_SLOT_LIMIT, orbital_count)
```

```python
import jax
import jax.numpy as jnp
from jax import lax
from jax.experimental import pallas as pl
from jax.experimental.pallas import tpu as pltpu
from jax.sharding import PartitionSpec as P

SIDE = 4
VMEM = 60 * 1024 * 1024


def pick_body(count_ref, cell_ref, orb_ref, out_ref, acc_ref):
    step = pl.program_id(0)
    part = orb_ref.shape[0]
    slots = out_ref.shape[0]
    wanted = jnp.transpose(jnp.broadcast_to(cell_ref[...], (slots, slots)))
    slot = lax.broadcasted_iota(jnp.int32, (slots, slots), 0)
    lane = lax.broadcasted_iota(jnp.int32, (slots, slots), 1)
    wanted = jnp.where(slot < count_ref[0], wanted, -1)
    hits = [
        (wanted == lane + (step * part + k * slots)).astype(jnp.float32).astype(jnp.bfloat16)
        for k in range(part // slots)
    ]
    term = jnp.dot(
        jnp.concatenate(hits, axis=1), orb_ref[...], preferred_element_type=jnp.float32
    )

    @pl.when(step == 0)
    def _():
        acc_ref[...] = term

    @pl.when(step > 0)
    def _():
        acc_ref[...] += term

    @pl.when(step == pl.num_programs(0) - 1)
    def _():
        out_ref[...] = acc_ref[...].astype(out_ref.dtype)


def pick(orbitals, cells, count):
    slab, width = orbitals.shape
    slots = cells.shape[1]
    part = 512
    return pl.pallas_call(
        pick_body,
        grid_spec=pltpu.PrefetchScalarGridSpec(
            num_scalar_prefetch=1,
            grid=(slab // part,),
            in_specs=[
                pl.BlockSpec((1, slots), lambda i, n: (0, 0)),
                pl.BlockSpec((part, width), lambda i, n: (i, 0)),
            ],
            out_specs=pl.BlockSpec((slots, width), lambda i, n: (0, 0)),
            scratch_shapes=[pltpu.VMEM((slots, width), jnp.float32)],
        ),
        out_shape=jax.ShapeDtypeStruct((slots, width), orbitals.dtype),
        compiler_params=pltpu.CompilerParams(vmem_limit_bytes=VMEM),
        name="pick",
    )(count, cells, orbitals)


def terms(groups, order, panel, tile, sizes, dtypes):
    rows = sum(g.shape[0] for g in groups)
    width = panel.shape[1]
    cols = panel.shape[0]
    slots = tile.shape[1]
    blocks = rows // slots
    col_part, out_part = 256, 640
    n_groups = len(groups)

    def body(order_ref, *refs):
        ins, rest = refs[:n_groups], refs[n_groups:]
        panel_ref, tiles, rest = rest[0], rest[1 : 1 + blocks], rest[1 + blocks :]
        outs, stacked, weighted = rest[: len(sizes)], rest[-2], rest[-1]
        at = 0
        for ref in ins:
            stacked[pl.ds(at, ref.shape[0]), :] = ref[...]
            at += ref.shape[0]
        for k in range(cols // col_part):
            span = pl.ds(k * col_part, col_part)
            gram = lax.dot_general(
                stacked[...],
                panel_ref[span, :],
                (((1,), (1,)), ((), ())),
                preferred_element_type=jnp.float32,
            )
            for j in range(blocks):
                part = gram[j * slots : (j + 1) * slots, :]
                weighted[pl.ds(j * slots, slots), span] = (
                    part * tiles[j][0, :, span].astype(jnp.float32)
                ).astype(jnp.bfloat16)
        for k in range(width // out_part):
            span = pl.ds(k * out_part, out_part)
            term = jnp.dot(weighted[...], panel_ref[:, span], preferred_element_type=jnp.float32)
            at = 0
            for ref, size in zip(outs, sizes):
                ref[:, span] = term[at : at + size, :].astype(ref.dtype)
                at += size

    def whole(shape):
        return pl.BlockSpec(shape, lambda i, o: (0, 0))

    def block_spec(j):
        return pl.BlockSpec((1, slots, cols), lambda i, o: (o[j], 0, 0))

    return pl.pallas_call(
        body,
        grid_spec=pltpu.PrefetchScalarGridSpec(
            num_scalar_prefetch=1,
            grid=(1,),
            in_specs=[whole(g.shape) for g in groups]
            + [whole(panel.shape)]
            + [block_spec(j) for j in range(blocks)],
            out_specs=[whole((size, width)) for size in sizes],
            scratch_shapes=[
                pltpu.VMEM((rows, width), jnp.bfloat16),
                pltpu.VMEM((rows, cols), jnp.bfloat16),
            ],
        ),
        out_shape=[jax.ShapeDtypeStruct((s, width), d) for s, d in zip(sizes, dtypes)],
        compiler_params=pltpu.CompilerParams(vmem_limit_bytes=VMEM),
        cost_estimate=pl.CostEstimate(
            flops=4 * rows * cols * width, bytes_accessed=8 * 1024 * 1024, transcendentals=0
        ),
        name="terms",
    )(order, *groups, panel, *([tile] * blocks))


def plane_perm(n_row, n_col, first, second):
    pairs = []
    for r in range(n_row):
        dx, dy = (first, second) if r % 2 == 0 else (second, first)
        for c in range(n_col):
            y, x = c // SIDE, c % SIDE
            to = ((y + dy) % SIDE) * SIDE + (x + dx) % SIDE
            pairs.append((r * n_col + c, r * n_col + to))
    return pairs


def solution(mesh):
    n_row, n_col = mesh.shape["row"], mesh.shape["col"]

    def first(a, by):
        return lax.ppermute(a, ("row", "col"), plane_perm(n_row, n_col, by, 0))

    def second(a, by):
        return lax.ppermute(a, ("row", "col"), plane_perm(n_row, n_col, 0, by))

    def on_device(orbitals, point_cell, point_count, kernel):
        slab, width = orbitals.shape
        slots = point_cell.shape[2]
        cells = lax.rem(point_cell.reshape(1, slots), slab)
        own = pick(orbitals, cells, point_count.reshape(1))

        panel = lax.all_gather(own, "row", axis=0, tiled=True)
        tile = kernel.reshape(n_col, slots, -1)

        core = lax.axis_index("row") % 2
        col = lax.axis_index("col")
        y, x = col // SIDE, col % SIDE

        def block_at(a, b):
            dx = jnp.where(core == 0, a, b)
            dy = jnp.where(core == 0, b, a)
            return ((y + dy) % SIDE) * SIDE + (x + dx) % SIDE

        def order_of(b, offsets=(0, -1, 1, 2)):
            return jnp.stack([block_at(a, b) for a in offsets]).astype(jnp.int32)

        low, high, far = first(own, 1), first(own, -1), first(own, 2)
        near = jnp.concatenate([own, low], axis=0)
        wide = jnp.concatenate([high, far], axis=0)
        near_low, wide_high = second(near, 1), second(wide, -1)
        wide_low, near_high = second(wide, 1), second(near, -1)
        near_far, wide_far = second(near_low, 1), second(wide_high, -1)

        bf, f32 = jnp.bfloat16, jnp.float32

        def reduced(group, b):
            mine, to_low, to_high, to_far = terms(
                group, order_of(b), panel, tile, (slots,) * 4, (f32, bf, bf, bf)
            )
            got = first(to_low, -1), first(to_high, 1), first(to_far, 2)
            return mine + got[0].astype(f32) + got[1].astype(f32) + got[2].astype(f32)

        here = reduced((near, wide), 0)
        to_low = reduced((near_low, wide_low), -1).astype(bf)
        to_high = reduced((near_high, wide_high), 1).astype(bf)
        to_far = reduced((near_far, wide_far), 2).astype(bf)
        got = second(to_low, -1), second(to_high, 1), second(to_far, 2)
        result = here + got[0].astype(f32) + got[1].astype(f32) + got[2].astype(f32)
        return result.reshape(1, 1, slots, width)

    in_specs = (
        P(("row", "col"), None),
        P("row", "col", None),
        P("row", "col"),
        P("row", None, None, None, "col", None),
    )
    out_specs = P("row", "col", None, None)
    return jax.shard_map(
        on_device, mesh=mesh, in_specs=in_specs, out_specs=out_specs, check_vma=False
    )
```

```python
import functools

import jax
import jax.numpy as jnp
from jax import lax
from jax.experimental import pallas as pl
from jax.experimental.pallas import tpu as pltpu
from jax.sharding import PartitionSpec as P

SIDE = 4
VMEM = 60 * 1024 * 1024


def pick_body(slab, count_ref, cell_ref, orb_ref, out_ref, acc_ref):
    step = pl.program_id(0)
    part = orb_ref.shape[0]
    slots = out_ref.shape[0]
    local = cell_ref[...] & (slab - 1)
    wanted = jnp.transpose(jnp.broadcast_to(local, (slots, slots)))
    slot = lax.broadcasted_iota(jnp.int32, (slots, slots), 0)
    lane = lax.broadcasted_iota(jnp.int32, (slots, slots), 1)
    wanted = jnp.where(slot < count_ref[0, 0], wanted, -1)
    hits = [
        (wanted == lane + (step * part + k * slots)).astype(jnp.float32).astype(jnp.bfloat16)
        for k in range(part // slots)
    ]
    term = jnp.dot(
        jnp.concatenate(hits, axis=1), orb_ref[...], preferred_element_type=jnp.float32
    )

    @pl.when(step == 0)
    def _():
        acc_ref[...] = term

    @pl.when(step > 0)
    def _():
        acc_ref[...] += term

    @pl.when(step == pl.num_programs(0) - 1)
    def _():
        out_ref[...] = acc_ref[...].astype(out_ref.dtype)


def pick(orbitals, cells, count):
    slab, width = orbitals.shape
    slots = cells.shape[1]
    part = 512
    assert slab & (slab - 1) == 0
    return pl.pallas_call(
        functools.partial(pick_body, slab),
        grid_spec=pltpu.PrefetchScalarGridSpec(
            num_scalar_prefetch=1,
            grid=(slab // part,),
            in_specs=[
                pl.BlockSpec((1, slots), lambda i, n: (0, 0)),
                pl.BlockSpec((part, width), lambda i, n: (i, 0)),
            ],
            out_specs=pl.BlockSpec((slots, width), lambda i, n: (0, 0)),
            scratch_shapes=[pltpu.VMEM((slots, width), jnp.float32)],
        ),
        out_shape=jax.ShapeDtypeStruct((slots, width), orbitals.dtype),
        compiler_params=pltpu.CompilerParams(vmem_limit_bytes=VMEM),
        name="pick",
    )(count, cells, orbitals)


def whole_arrays(body, ins, outs, after=(), behind=(), scalars=(), scratch=(), flops=0, name=None):
    vmem = pl.BlockSpec(memory_space=pltpu.VMEM)
    smem = pl.BlockSpec(memory_space=pltpu.SMEM)
    held = pl.BlockSpec(memory_space=pl.ANY)

    def run(*refs):
        n, m = len(scalars) + len(ins), len(after) + len(behind)
        mark = refs[n + m + len(outs)]
        mark[...] = jnp.zeros_like(mark)
        body(*refs[:n], *refs[n + m : n + m + len(outs)], *refs[n + m + len(outs) + 1 :])

    outs = list(outs)
    marks = [((8, 128), jnp.int32)]

    return pl.pallas_call(
        run,
        in_specs=[smem] * len(scalars) + [vmem] * (len(ins) + len(after)) + [held] * len(behind),
        out_specs=[vmem] * (len(outs) + 1),
        out_shape=[jax.ShapeDtypeStruct(shape, dtype) for shape, dtype in outs + marks],
        scratch_shapes=scratch,
        compiler_params=pltpu.CompilerParams(vmem_limit_bytes=30 * 1024 * 1024),
        cost_estimate=pl.CostEstimate(flops=flops, bytes_accessed=1024, transcendentals=0),
        name=name,
    )(*scalars, *ins, *after, *behind)


def terms(groups, order, panels, tile, outs, after=()):
    width = panels[0].shape[1]
    depth = panels[0].shape[0]
    cols = depth * len(panels)
    slots = tile.shape[1]
    sizes = [g.shape[0] for g in groups]
    blocks = sum(sizes) // slots
    col_part, out_part = 256, 640
    n_groups, n_panels = len(groups), len(panels)
    batch = 512

    def body(order_ref, *refs):
        ins, refs = refs[:n_groups], refs[n_groups:]
        panel_refs, refs = refs[:n_panels], refs[n_panels:]
        tile_ref, refs = refs[0], refs[1:]
        out_refs, (weighted, rows) = refs[: len(outs)], refs[len(outs) :]
        top = 0
        for ref, size in zip(ins, sizes):
            rows[pl.ds(top, size), :] = ref[...]
            top += size
        for k in range(cols // col_part):
            panel_ref = panel_refs[k * col_part // depth]
            for top in range(0, sum(sizes), batch):
                gram = lax.dot_general(
                    rows[pl.ds(top, batch), :],
                    panel_ref[pl.ds(k * col_part % depth, col_part), :],
                    (((1,), (1,)), ((), ())),
                    preferred_element_type=jnp.float32,
                )
                for j in range(batch // slots):
                    span = pl.ds(k * col_part, col_part)
                    part = gram[j * slots : (j + 1) * slots, :]
                    kern = tile_ref[order_ref[top // slots + j], :, span].astype(jnp.float32)
                    weighted[pl.ds(top + j * slots, slots), span] = (part * kern).astype(
                        jnp.bfloat16
                    )
        for k in range(width // out_part):
            span = pl.ds(k * out_part, out_part)
            term = None
            for i, panel_ref in enumerate(panel_refs):
                more = jnp.dot(
                    weighted[:, pl.ds(i * depth, depth)],
                    panel_ref[:, span],
                    preferred_element_type=jnp.float32,
                )
                term = more if term is None else term + more
            for ref, (dtype, parts) in zip(out_refs, outs):
                at = 0
                for block, start, size in parts:
                    top = block * slots + start
                    ref[pl.ds(at, size), span] = term[top : top + size, :].astype(dtype)
                    at += size

    return whole_arrays(
        body,
        (*groups, *panels, tile),
        [((sum(p[2] for p in parts), width), dtype) for dtype, parts in outs],
        after=after,
        scalars=(order,),
        scratch=[pltpu.VMEM((sum(sizes), n), jnp.bfloat16) for n in (cols, width)],
        flops=4 * sum(sizes) * cols * width,
        name="terms",
    )


def stack(*ins, after=()):
    rows, width = sum(a.shape[0] for a in ins), ins[0].shape[1]

    def body(*refs):
        top = 0
        for ref in refs[: len(ins)]:
            refs[len(ins)][pl.ds(top, ref.shape[0]), :] = ref[...]
            top += ref.shape[0]

    return whole_arrays(body, ins, [((rows, width), ins[0].dtype)], after=after, name="stack")


def sums(mine, got, cuts, dtype, after=(), behind=()):
    rows, width = mine.shape
    size = rows // cuts

    def body(*refs):
        ins, outs = refs[: 1 + len(got)], refs[1 + len(got) :]
        for k, out in enumerate(outs):
            span = pl.ds(k * size, size)
            total = ins[0][span, :].astype(jnp.float32)
            for ref in ins[1:]:
                total = total + ref[span, :].astype(jnp.float32)
            out[...] = total.astype(dtype)

    outs = [((size, width), dtype)] * cuts
    return whole_arrays(body, (mine, *got), outs, after=after, behind=behind, name="sums")


def plane_perm(n_row, n_col, first, second):
    pairs = []
    for r in range(n_row):
        dx, dy = (first, second) if r % 2 == 0 else (second, first)
        for c in range(n_col):
            y, x = c // SIDE, c % SIDE
            to = ((y + dy) % SIDE) * SIDE + (x + dx) % SIDE
            pairs.append((r * n_col + c, r * n_col + to))
    return pairs


def solution(mesh):
    n_row, n_col = mesh.shape["row"], mesh.shape["col"]
    bf, f32 = jnp.bfloat16, jnp.float32

    def first(a, by):
        return lax.ppermute(a, ("row", "col"), plane_perm(n_row, n_col, by, 0))

    def second(a, by):
        return lax.ppermute(a, ("row", "col"), plane_perm(n_row, n_col, 0, by))

    def on_device(orbitals, point_cell, point_count, kernel):
        slab, width = orbitals.shape
        slots = point_cell.shape[2]
        own = pick(orbitals, point_cell.reshape(1, slots), point_count)
        tile = kernel.reshape(n_col, slots, -1)

        offsets = (0, -1, 1, 2)
        low, high, far = first(own, 1), first(own, -1), first(own, 2)
        near, mark = stack(own, low)
        near_low, near_high = second(near, 1), second(near, -1)
        wide, _ = stack(high, far, after=(mark,))
        wide_low, wide_high = second(wide, 1), second(wide, -1)
        panels = (lax.all_gather(own, "row", axis=0, tiled=True),)

        row, col = lax.axis_index("row"), lax.axis_index("col")
        core, y, x = row % 2, col // SIDE, col % SIDE

        def terms_of(groups, bs, after=()):
            blocks = []
            for b in bs:
                for a in offsets:
                    dx, dy = jnp.where(core == 0, a, b), jnp.where(core == 0, b, a)
                    blocks.append(((y + dy) % SIDE) * SIDE + (x + dx) % SIDE)
            order = jnp.stack(blocks).astype(jnp.int32)
            outs = [
                (f32 if k == 0 else bf, [(4 * i + k, 0, slots) for i in range(len(bs))])
                for k in range(4)
            ]
            return terms(groups, order, panels, tile, outs, after=after)

        def over_first(t):
            return first(t[1], -1), first(t[2], 1), first(t[3], 2)

        def total(mine, got):
            return mine + sum(a.astype(f32) for a in got)

        *t_here, mark = terms_of((near, wide), (0,))
        got_here = over_first(t_here)
        near_far, wide_far = second(near_low, 1), second(wide_high, -1)
        *t_near, mark = terms_of((near_low, wide_low, near_high, wide_high), (-1, 1), after=(mark,))
        here, mark = sums(t_here[0], got_here, 1, f32, after=(mark,))
        got_near = over_first(t_near)
        *t_far, mark = terms_of((near_far, wide_far), (2,), after=(mark,))
        got_far = over_first(t_far)
        to_low, to_high, mark = sums(t_near[0], got_near, 2, bf, after=(mark,))
        got = second(to_low, -1), second(to_high, 1)
        to_far, _ = sums(t_far[0], got_far, 1, bf, after=(mark,), behind=got)
        result = total(here, (*got, second(to_far, 2)))
        return result.reshape(1, 1, slots, width)

    in_specs = (
        P(("row", "col"), None),
        P("row", "col", None),
        P("row", "col"),
        P("row", None, None, None, "col", None),
    )
    out_specs = P("row", "col", None, None)
    return jax.shard_map(
        on_device, mesh=mesh, in_specs=in_specs, out_specs=out_specs, check_vma=False
    )
```

```python
import functools

import jax
import jax.numpy as jnp
from jax import lax
from jax.experimental import pallas as pl
from jax.experimental.pallas import tpu as pltpu
from jax.sharding import PartitionSpec as P

SIDE = 4
VMEM = 60 * 1024 * 1024


def pick_body(slab, count_ref, order_ref, cell_ref, orb_ref, out_ref, acc_ref):
    step = pl.program_id(0)
    part = orb_ref.shape[0]
    slots = out_ref.shape[0]
    local = cell_ref[...] & (slab - 1)
    wanted = jnp.transpose(jnp.broadcast_to(local, (slots, slots)))
    slot = lax.broadcasted_iota(jnp.int32, (slots, slots), 0)
    lane = lax.broadcasted_iota(jnp.int32, (slots, slots), 1)
    wanted = jnp.where(slot < count_ref[0, 0], wanted, -1)
    hits = [
        (wanted == lane + (step * part + k * slots)).astype(jnp.float32).astype(jnp.bfloat16)
        for k in range(part // slots)
    ]
    term = jnp.dot(
        jnp.concatenate(hits, axis=1), orb_ref[...], preferred_element_type=jnp.float32
    )

    @pl.when(step == 0)
    def _():
        acc_ref[...] = term

    @pl.when(step > 0)
    def _():
        acc_ref[...] += term

    @pl.when(step == pl.num_programs(0) - 1)
    def _():
        out_ref[...] = acc_ref[...].astype(out_ref.dtype)


def pick(orbitals, cells, count, order):
    slab, width = orbitals.shape
    slots = cells.shape[1]
    part = 512
    assert slab & (slab - 1) == 0
    return pl.pallas_call(
        functools.partial(pick_body, slab),
        grid_spec=pltpu.PrefetchScalarGridSpec(
            num_scalar_prefetch=2,
            grid=(slab // part,),
            in_specs=[
                pl.BlockSpec((1, slots), lambda i, n, o: (0, 0)),
                pl.BlockSpec((part, width), lambda i, n, o: (i, 0)),
            ],
            out_specs=pl.BlockSpec((slots, width), lambda i, n, o: (0, 0)),
            scratch_shapes=[pltpu.VMEM((slots, width), jnp.float32)],
        ),
        out_shape=jax.ShapeDtypeStruct((slots, width), orbitals.dtype),
        compiler_params=pltpu.CompilerParams(vmem_limit_bytes=VMEM),
        name="pick",
    )(count, order, cells, orbitals)


def whole_arrays(body, ins, outs, after=(), behind=(), scalars=(), scratch=(), flops=0, name=None):
    vmem = pl.BlockSpec(memory_space=pltpu.VMEM)
    smem = pl.BlockSpec(memory_space=pltpu.SMEM)
    held = pl.BlockSpec(memory_space=pl.ANY)

    def run(*refs):
        n, m = len(scalars) + len(ins), len(after) + len(behind)
        mark = refs[n + m + len(outs)]
        mark[...] = jnp.zeros_like(mark)
        body(*refs[:n], *refs[n + m : n + m + len(outs)], *refs[n + m + len(outs) + 1 :])

    outs = list(outs)
    marks = [((8, 128), jnp.int32)]

    return pl.pallas_call(
        run,
        in_specs=[smem] * len(scalars) + [vmem] * (len(ins) + len(after)) + [held] * len(behind),
        out_specs=[vmem] * (len(outs) + 1),
        out_shape=[jax.ShapeDtypeStruct(shape, dtype) for shape, dtype in outs + marks],
        scratch_shapes=scratch,
        compiler_params=pltpu.CompilerParams(vmem_limit_bytes=16 * 1024 * 1024),
        cost_estimate=pl.CostEstimate(flops=flops, bytes_accessed=1024, transcendentals=0),
        name=name,
    )(*scalars, *ins, *after, *behind)


def terms(groups, order, first_block, panels, tile, outs, after=()):
    width = panels[0].shape[1]
    depth = panels[0].shape[0]
    cols = depth * len(panels)
    slots = tile.shape[1]
    sizes = [g.shape[0] for g in groups]
    col_part, out_part = 256, 640
    n_groups, n_panels = len(groups), len(panels)

    def body(order_ref, *refs):
        ins, refs = refs[:n_groups], refs[n_groups:]
        panel_refs, refs = refs[:n_panels], refs[n_panels:]
        tile_ref, refs = refs[0], refs[1:]
        out_refs, (weighted,) = refs[: len(outs)], refs[len(outs) :]
        for k in range(cols // col_part):
            panel_ref = panel_refs[k * col_part // depth]
            top = 0
            for ref, size in zip(ins, sizes):
                gram = lax.dot_general(
                    ref[...],
                    panel_ref[pl.ds(k * col_part % depth, col_part), :],
                    (((1,), (1,)), ((), ())),
                    preferred_element_type=jnp.float32,
                )
                for j in range(size // slots):
                    span = pl.ds(k * col_part, col_part)
                    part = gram[j * slots : (j + 1) * slots, :]
                    kern = tile_ref[order_ref[first_block + top // slots + j], :, span].astype(jnp.float32)
                    weighted[pl.ds(top + j * slots, slots), span] = (part * kern).astype(
                        jnp.bfloat16
                    )
                top += size
        for k in range(width // out_part):
            span = pl.ds(k * out_part, out_part)
            term = None
            for i, panel_ref in enumerate(panel_refs):
                more = jnp.dot(
                    weighted[:, pl.ds(i * depth, depth)],
                    panel_ref[:, span],
                    preferred_element_type=jnp.float32,
                )
                term = more if term is None else term + more
            for ref, (dtype, parts) in zip(out_refs, outs):
                at = 0
                for block, start, size in parts:
                    top = block * slots + start
                    ref[pl.ds(at, size), span] = term[top : top + size, :].astype(dtype)
                    at += size

    return whole_arrays(
        body,
        (*groups, *panels, tile),
        [((sum(p[2] for p in parts), width), dtype) for dtype, parts in outs],
        after=after,
        scalars=(order,),
        scratch=[pltpu.VMEM((sum(sizes), cols), jnp.bfloat16)],
        flops=4 * sum(sizes) * cols * width,
        name="terms",
    )


def stacks(pieces, after=(), behind=()):
    ins = [a for parts in pieces for a in parts]
    rows = [sum(a.shape[0] for a in parts) for parts in pieces]

    def body(*refs):
        i = 0
        for out, parts in zip(refs[len(ins) :], pieces):
            top = 0
            for a in parts:
                out[pl.ds(top, a.shape[0]), :] = refs[i][...]
                top += a.shape[0]
                i += 1

    outs = [((n, ins[0].shape[1]), ins[0].dtype) for n in rows]
    return whole_arrays(body, ins, outs, after=after, behind=behind, name="stacks")


def place(ins, order, first_place, slots, after=(), behind=()):
    rows, width = sum(a.shape[0] for a in ins), ins[0].shape[1]

    def body(order_ref, *refs):
        i = 0
        for ref, a in zip(refs, ins):
            for start in range(0, a.shape[0], slots):
                at = pl.multiple_of(order_ref[first_place + i] * slots, slots)
                refs[len(ins)][pl.ds(at, slots), :] = ref[pl.ds(start, slots), :]
                i += 1

    outs = [((rows, width), ins[0].dtype)]
    return whole_arrays(body, ins, outs, after=after, behind=behind, scalars=(order,), name="place")


def sums(mine, got, cuts, dtype, after=(), behind=()):
    rows, width = mine.shape
    size = rows // cuts

    def body(*refs):
        ins, outs = refs[: 1 + len(got)], refs[1 + len(got) :]
        for k, out in enumerate(outs):
            span = pl.ds(k * size, size)
            total = ins[0][span, :].astype(jnp.float32)
            for ref in ins[1:]:
                total = total + ref[span, :].astype(jnp.float32)
            out[...] = total.astype(dtype)

    outs = [((size, width), dtype)] * cuts
    return whole_arrays(body, (mine, *got), outs, after=after, behind=behind, name="sums")


def plane_perm(n_row, n_col, first, second):
    pairs = []
    for r in range(n_row):
        dx, dy = (first, second) if r % 2 == 0 else (second, first)
        for c in range(n_col):
            y, x = c // SIDE, c % SIDE
            to = ((y + dy) % SIDE) * SIDE + (x + dx) % SIDE
            pairs.append((r * n_col + c, r * n_col + to))
    return pairs


def solution(mesh):
    n_row, n_col = mesh.shape["row"], mesh.shape["col"]
    bf, f32 = jnp.bfloat16, jnp.float32

    def first(a, by):
        return lax.ppermute(a, ("row", "col"), plane_perm(n_row, n_col, by, 0))

    def second(a, by):
        return lax.ppermute(a, ("row", "col"), plane_perm(n_row, n_col, 0, by))

    def other_core(a):
        return lax.ppermute(a, "row", [(r, r ^ 1) for r in range(n_row)])

    def around_z(a):
        to = [(r + 2 - 4 * (r % 2)) % n_row for r in range(n_row)]
        return lax.ppermute(a, "row", list(enumerate(to)))

    def on_device(orbitals, point_cell, point_count, kernel):
        slab, width = orbitals.shape
        slots = point_cell.shape[2]

        offsets = (0, -1, 1, 2)
        row, col = lax.axis_index("row"), lax.axis_index("col")
        z, core, y, x = row // 2, row % 2, col // SIDE, col % SIDE
        order = []
        for b in offsets:
            for a in offsets:
                dx, dy = jnp.where(core == 0, a, b), jnp.where(core == 0, b, a)
                order.append(((y + dy) % SIDE) * SIDE + (x + dx) % SIDE)
        for of in (core, 1 - core):
            order += [2 * ((z + (2 * of - 1) * step + SIDE) % SIDE) + of for step in range(SIDE)]
        order = jnp.stack(order).astype(jnp.int32)

        own = pick(orbitals, point_cell.reshape(1, slots), point_count, order)
        tile = kernel.reshape(n_col, slots, -1)
        low, high, far = first(own, 1), first(own, -1), first(own, 2)
        along = [own]
        for _ in range(SIDE - 1):
            along.append(around_z(along[-1]))
        near, wide, mark = stacks(((own, low), (high, far)))
        near_low, wide_high = second(near, 1), second(wide, -1)
        wide_low, near_high = second(wide, 1), second(near, -1)
        mine, mark = stacks((along,), after=(mark,), behind=(near_low, wide_high, tile))
        panel, mark = place(
            (mine, other_core(mine)),
            order,
            SIDE * SIDE,
            slots,
            after=(mark,),
        )

        def terms_of(groups, bs, after=()):
            outs = [
                (f32 if k == 0 else bf, [(4 * i + k, 0, slots) for i in range(len(bs))])
                for k in range(4)
            ]
            at = SIDE * offsets.index(bs[0])
            return terms(groups, order, at, (panel,), tile, outs, after=after)

        def over_first(t):
            far = first(t[3], 2)
            return far, first(t[1], -1), first(t[2], 1)

        def total(mine, got):
            return mine + sum(a.astype(f32) for a in got)

        *t_here, mark = terms_of((near, wide), (0,), after=(mark,))
        got_here = over_first(t_here)
        near_far, wide_far = second(near_low, 1), second(wide_high, -1)
        *t_near, mark = terms_of((near_low, wide_low, near_high, wide_high), (-1, 1), after=(mark,))
        here, mark = sums(t_here[0], got_here, 1, f32, after=(mark,))
        got_near = over_first(t_near)
        *t_far, mark = terms_of((near_far, wide_far), (2,), after=(mark,))
        got_far = over_first(t_far)
        to_low, to_high, mark = sums(t_near[0], got_near, 2, bf, after=(mark,))
        got = second(to_low, -1), second(to_high, 1)
        to_far, _ = sums(t_far[0], got_far, 1, bf, after=(mark,), behind=got)
        result = total(here, (*got, second(to_far, 2)))
        return result.reshape(1, 1, slots, width)

    in_specs = (
        P(("row", "col"), None),
        P("row", "col", None),
        P("row", "col"),
        P("row", None, None, None, "col", None),
    )
    out_specs = P("row", "col", None, None)
    return jax.shard_map(
        on_device, mesh=mesh, in_specs=in_specs, out_specs=out_specs, check_vma=False
    )
```

```python
import functools

import jax
import jax.numpy as jnp
from jax import lax
from jax.experimental import pallas as pl
from jax.experimental.pallas import tpu as pltpu
from jax.sharding import PartitionSpec as P

SIDE = 4
VMEM = 60 * 1024 * 1024


def pick_body(slab, count_ref, order_ref, cell_ref, orb_ref, out_ref, acc_ref):
    step = pl.program_id(0)
    part = orb_ref.shape[0]
    slots = out_ref.shape[0]
    local = cell_ref[...] & (slab - 1)
    wanted = jnp.transpose(jnp.broadcast_to(local, (slots, slots)))
    slot = lax.broadcasted_iota(jnp.int32, (slots, slots), 0)
    lane = lax.broadcasted_iota(jnp.int32, (slots, slots), 1)
    wanted = jnp.where(slot < count_ref[0, 0], wanted, -1)
    hits = [
        (wanted == lane + (step * part + k * slots)).astype(jnp.float32).astype(jnp.bfloat16)
        for k in range(part // slots)
    ]
    term = jnp.dot(
        jnp.concatenate(hits, axis=1), orb_ref[...], preferred_element_type=jnp.float32
    )

    @pl.when(step == 0)
    def _():
        acc_ref[...] = term

    @pl.when(step > 0)
    def _():
        acc_ref[...] += term

    @pl.when(step == pl.num_programs(0) - 1)
    def _():
        out_ref[...] = acc_ref[...].astype(out_ref.dtype)


def pick(orbitals, cells, count, order):
    slab, width = orbitals.shape
    slots = cells.shape[1]
    part = 1024
    assert slab & (slab - 1) == 0
    return pl.pallas_call(
        functools.partial(pick_body, slab),
        grid_spec=pltpu.PrefetchScalarGridSpec(
            num_scalar_prefetch=2,
            grid=(slab // part,),
            in_specs=[
                pl.BlockSpec((1, slots), lambda i, n, o: (0, 0)),
                pl.BlockSpec((part, width), lambda i, n, o: (i, 0)),
            ],
            out_specs=pl.BlockSpec((slots, width), lambda i, n, o: (0, 0)),
            scratch_shapes=[pltpu.VMEM((slots, width), jnp.float32)],
        ),
        out_shape=jax.ShapeDtypeStruct((slots, width), orbitals.dtype),
        compiler_params=pltpu.CompilerParams(vmem_limit_bytes=VMEM),
        name="pick",
    )(count, order, cells, orbitals)


def whole_arrays(body, ins, outs, after=(), behind=(), scalars=(), scratch=(), flops=0, name=None):
    vmem = pl.BlockSpec(memory_space=pltpu.VMEM)
    smem = pl.BlockSpec(memory_space=pltpu.SMEM)
    held = pl.BlockSpec(memory_space=pl.ANY)

    def run(*refs):
        n, m = len(scalars) + len(ins), len(after) + len(behind)
        mark = refs[n + m + len(outs)]
        mark[...] = jnp.zeros_like(mark)
        body(*refs[:n], *refs[n + m : n + m + len(outs)], *refs[n + m + len(outs) + 1 :])

    outs = list(outs)
    marks = [((8, 128), jnp.int32)]

    return pl.pallas_call(
        run,
        in_specs=[smem] * len(scalars) + [vmem] * (len(ins) + len(after)) + [held] * len(behind),
        out_specs=[vmem] * (len(outs) + 1),
        out_shape=[jax.ShapeDtypeStruct(shape, dtype) for shape, dtype in outs + marks],
        scratch_shapes=scratch,
        compiler_params=pltpu.CompilerParams(vmem_limit_bytes=16 * 1024 * 1024),
        cost_estimate=pl.CostEstimate(flops=flops, bytes_accessed=1024, transcendentals=0),
        name=name,
    )(*scalars, *ins, *after, *behind)


def relayout(kernel):
    rows, outer, inner = kernel.shape
    part = 512

    def body(in_ref, out_ref, mark_ref, wide_ref):
        mark_ref[...] = jnp.zeros_like(mark_ref)
        wide_ref[...] = in_ref[...].astype(jnp.float32).reshape(wide_ref.shape)
        span = pl.ds(pl.multiple_of(pl.program_id(0) * part, part), part)
        for r in range(outer):
            piece = wide_ref[pl.ds(r, part, stride=outer), :]
            out_ref[span, pl.ds(r * inner, inner)] = piece.astype(out_ref.dtype)

    vmem = pl.BlockSpec(memory_space=pltpu.VMEM)
    return pl.pallas_call(
        body,
        grid=(rows // part,),
        in_specs=[pl.BlockSpec((part, outer, inner), lambda i: (i, 0, 0))],
        out_specs=[vmem, vmem],
        out_shape=[
            jax.ShapeDtypeStruct((rows, outer * inner), kernel.dtype),
            jax.ShapeDtypeStruct((8, 128), jnp.int32),
        ],
        scratch_shapes=[pltpu.VMEM((part * outer, inner), jnp.float32)],
        compiler_params=pltpu.CompilerParams(vmem_limit_bytes=16 * 1024 * 1024),
        cost_estimate=pl.CostEstimate(flops=0, bytes_accessed=1024, transcendentals=0),
        name="relayout",
    )(kernel)


def terms(groups, order, first_block, panels, tile, outs, after=()):
    width = panels[0].shape[1]
    depth = panels[0].shape[0]
    cols = depth * len(panels)
    slots = tile.shape[1]
    sizes = [g.shape[0] for g in groups]
    col_part, out_part = 256, 640
    n_groups, n_panels = len(groups), len(panels)

    def body(order_ref, *refs):
        ins, refs = refs[:n_groups], refs[n_groups:]
        panel_refs, refs = refs[:n_panels], refs[n_panels:]
        tile_ref, refs = refs[0], refs[1:]
        out_refs, (weighted,) = refs[: len(outs)], refs[len(outs) :]
        for k in range(cols // col_part):
            panel_ref = panel_refs[k * col_part // depth]
            top = 0
            for ref, size in zip(ins, sizes):
                gram = lax.dot_general(
                    ref[...],
                    panel_ref[pl.ds(k * col_part % depth, col_part), :],
                    (((1,), (1,)), ((), ())),
                    preferred_element_type=jnp.float32,
                )
                for j in range(size // slots):
                    span = pl.ds(k * col_part, col_part)
                    part = gram[j * slots : (j + 1) * slots, :]
                    kern = tile_ref[order_ref[first_block + top // slots + j], :, span].astype(jnp.float32)
                    weighted[pl.ds(top + j * slots, slots), span] = (part * kern).astype(
                        jnp.bfloat16
                    )
                top += size
        for k in range(width // out_part):
            span = pl.ds(k * out_part, out_part)
            term = None
            for i, panel_ref in enumerate(panel_refs):
                more = jnp.dot(
                    weighted[:, pl.ds(i * depth, depth)],
                    panel_ref[:, span],
                    preferred_element_type=jnp.float32,
                )
                term = more if term is None else term + more
            for ref, (dtype, parts) in zip(out_refs, outs):
                at = 0
                for block, start, size in parts:
                    top = block * slots + start
                    ref[pl.ds(at, size), span] = term[top : top + size, :].astype(dtype)
                    at += size

    return whole_arrays(
        body,
        (*groups, *panels, tile),
        [((sum(p[2] for p in parts), width), dtype) for dtype, parts in outs],
        after=after,
        scalars=(order,),
        scratch=[pltpu.VMEM((sum(sizes), cols), jnp.bfloat16)],
        flops=4 * sum(sizes) * cols * width,
        name="terms",
    )


def stacks(pieces, after=(), behind=()):
    ins = [a for parts in pieces for a in parts]
    rows = [sum(a.shape[0] for a in parts) for parts in pieces]

    def body(*refs):
        i = 0
        for out, parts in zip(refs[len(ins) :], pieces):
            top = 0
            for a in parts:
                out[pl.ds(top, a.shape[0]), :] = refs[i][...]
                top += a.shape[0]
                i += 1

    outs = [((n, ins[0].shape[1]), ins[0].dtype) for n in rows]
    return whole_arrays(body, ins, outs, after=after, behind=behind, name="stacks")


def place(ins, order, first_place, slots, after=(), behind=()):
    rows, width = sum(a.shape[0] for a in ins), ins[0].shape[1]

    def body(order_ref, *refs):
        i = 0
        for ref, a in zip(refs, ins):
            for start in range(0, a.shape[0], slots):
                at = pl.multiple_of(order_ref[first_place + i] * slots, slots)
                refs[len(ins)][pl.ds(at, slots), :] = ref[pl.ds(start, slots), :]
                i += 1

    outs = [((rows, width), ins[0].dtype)]
    return whole_arrays(body, ins, outs, after=after, behind=behind, scalars=(order,), name="place")


def sums(mine, got, cuts, dtype, after=(), behind=()):
    rows, width = mine.shape
    size = rows // cuts

    def body(*refs):
        ins, outs = refs[: 1 + len(got)], refs[1 + len(got) :]
        for k, out in enumerate(outs):
            span = pl.ds(k * size, size)
            total = ins[0][span, :].astype(jnp.float32)
            for ref in ins[1:]:
                total = total + ref[span, :].astype(jnp.float32)
            out[...] = total.astype(dtype)

    outs = [((size, width), dtype)] * cuts
    return whole_arrays(body, (mine, *got), outs, after=after, behind=behind, name="sums")


def plane_perm(n_row, n_col, first, second):
    pairs = []
    for r in range(n_row):
        dx, dy = (first, second) if r % 2 == 0 else (second, first)
        for c in range(n_col):
            y, x = c // SIDE, c % SIDE
            to = ((y + dy) % SIDE) * SIDE + (x + dx) % SIDE
            pairs.append((r * n_col + c, r * n_col + to))
    return pairs


def solution(mesh):
    n_row, n_col = mesh.shape["row"], mesh.shape["col"]
    bf, f32 = jnp.bfloat16, jnp.float32

    def first(a, by):
        return lax.ppermute(a, ("row", "col"), plane_perm(n_row, n_col, by, 0))

    def second(a, by):
        return lax.ppermute(a, ("row", "col"), plane_perm(n_row, n_col, 0, by))

    def other_core(a):
        return lax.ppermute(a, "row", [(r, r ^ 1) for r in range(n_row)])

    def around_z(a):
        to = [(r + 2 - 4 * (r % 2)) % n_row for r in range(n_row)]
        return lax.ppermute(a, "row", list(enumerate(to)))

    def on_device(orbitals, point_cell, point_count, kernel):
        slab, width = orbitals.shape
        slots = point_cell.shape[2]

        offsets, b_offsets = (2, 1, -1, 0), (0, -1, 1, 2)
        row, col = lax.axis_index("row"), lax.axis_index("col")
        z, core, y, x = row // 2, row % 2, col // SIDE, col % SIDE
        order = []
        for b in b_offsets:
            for a in offsets:
                dx, dy = jnp.where(core == 0, a, b), jnp.where(core == 0, b, a)
                order.append(((y + dy) % SIDE) * SIDE + (x + dx) % SIDE)
        for of in (core, 1 - core):
            order += [2 * ((z + (2 * of - 1) * step + SIDE) % SIDE) + of for step in range(SIDE)]
        order = jnp.stack(order).astype(jnp.int32)

        own = pick(orbitals, point_cell.reshape(1, slots), point_count, order)
        tile, mark = relayout(kernel.reshape(n_col * slots, n_row, slots))
        tile = tile.reshape(n_col, slots, -1)
        far = first(own, 2)
        low, high = first(own, 1), first(own, -1)
        along = [own]
        for _ in range(SIDE - 1):
            along.append(around_z(along[-1]))
        wide, near, mark = stacks(((far, high), (low, own)), after=(mark,))
        near_low, wide_high = second(near, 1), second(wide, -1)
        wide_low, near_high = second(wide, 1), second(near, -1)
        mine, mark = stacks((along,), after=(mark,), behind=(near_low, wide_high))
        panel, mark = place(
            (mine, other_core(mine)),
            order,
            SIDE * SIDE,
            slots,
            after=(mark,),
        )

        def terms_of(groups, bs, after=()):
            outs = [
                (f32 if a == 0 else bf, [(4 * i + k, 0, slots) for i in range(len(bs))])
                for k, a in enumerate(offsets)
            ]
            at = SIDE * b_offsets.index(bs[0])
            return terms(groups, order, at, (panel,), tile, outs, after=after)

        def over_first(t):
            return first(t[0], 2), first(t[1], 1), first(t[2], -1)

        def total(mine, got):
            return mine + sum(a.astype(f32) for a in got)

        *t_here, mark = terms_of((wide, near), (0,), after=(mark,))
        got_here = over_first(t_here)
        near_far, wide_far = second(near_low, 1), second(wide_high, -1)
        *t_near, mark = terms_of((wide_low, near_low, wide_high, near_high), (-1, 1), after=(mark,))
        here, mark = sums(t_here[3], got_here, 1, f32, after=(mark,))
        got_near = over_first(t_near)
        *t_far, mark = terms_of((wide_far, near_far), (2,), after=(mark,))
        got_far = over_first(t_far)
        to_low, to_high, mark = sums(t_near[3], got_near, 2, bf, after=(mark,))
        got = second(to_low, -1), second(to_high, 1)
        to_far, _ = sums(t_far[3], got_far, 1, bf, after=(mark,), behind=got)
        result = total(here, (*got, second(to_far, 2)))
        return result.reshape(1, 1, slots, width)

    in_specs = (
        P(("row", "col"), None),
        P("row", "col", None),
        P("row", "col"),
        P("row", None, None, None, "col", None),
    )
    out_specs = P("row", "col", None, None)
    return jax.shard_map(
        on_device, mesh=mesh, in_specs=in_specs, out_specs=out_specs, check_vma=False
    )
```

```python
import functools

import jax
import jax.numpy as jnp
from jax import lax
from jax.experimental import pallas as pl
from jax.experimental.pallas import tpu as pltpu
from jax.sharding import PartitionSpec as P

SIDE = 4
VMEM = 60 * 1024 * 1024


def pick_body(slab, count_ref, order_ref, cell_ref, orb_ref, out_ref, acc_ref):
    step = pl.program_id(0)
    part = orb_ref.shape[0]
    slots = out_ref.shape[0]
    local = cell_ref[...] & (slab - 1)
    wanted = jnp.transpose(jnp.broadcast_to(local, (slots, slots)))
    slot = lax.broadcasted_iota(jnp.int32, (slots, slots), 0)
    lane = lax.broadcasted_iota(jnp.int32, (slots, slots), 1)
    wanted = jnp.where(slot < count_ref[0, 0], wanted, -1)
    hits = [
        (wanted == lane + (step * part + k * slots)).astype(jnp.float32).astype(jnp.bfloat16)
        for k in range(part // slots)
    ]
    term = jnp.dot(
        jnp.concatenate(hits, axis=1), orb_ref[...], preferred_element_type=jnp.float32
    )

    @pl.when(step == 0)
    def _():
        acc_ref[...] = term

    @pl.when(step > 0)
    def _():
        acc_ref[...] += term

    @pl.when(step == pl.num_programs(0) - 1)
    def _():
        out_ref[...] = acc_ref[...].astype(out_ref.dtype)


def pick(orbitals, cells, count, order):
    slab, width = orbitals.shape
    slots = cells.shape[1]
    part = 1024
    assert slab & (slab - 1) == 0
    return pl.pallas_call(
        functools.partial(pick_body, slab),
        grid_spec=pltpu.PrefetchScalarGridSpec(
            num_scalar_prefetch=2,
            grid=(slab // part,),
            in_specs=[
                pl.BlockSpec((1, slots), lambda i, n, o: (0, 0)),
                pl.BlockSpec((part, width), lambda i, n, o: (i, 0)),
            ],
            out_specs=pl.BlockSpec((slots, width), lambda i, n, o: (0, 0)),
            scratch_shapes=[pltpu.VMEM((slots, width), jnp.float32)],
        ),
        out_shape=jax.ShapeDtypeStruct((slots, width), orbitals.dtype),
        compiler_params=pltpu.CompilerParams(vmem_limit_bytes=VMEM),
        name="pick",
    )(count, order, cells, orbitals)


def whole_arrays(body, ins, outs, after=(), behind=(), scalars=(), scratch=(), flops=0, name=None):
    vmem = pl.BlockSpec(memory_space=pltpu.VMEM)
    smem = pl.BlockSpec(memory_space=pltpu.SMEM)
    held = pl.BlockSpec(memory_space=pl.ANY)

    def run(*refs):
        n, m = len(scalars) + len(ins), len(after) + len(behind)
        mark = refs[n + m + len(outs)]
        mark[...] = jnp.zeros_like(mark)
        body(*refs[:n], *refs[n + m : n + m + len(outs)], *refs[n + m + len(outs) + 1 :])

    outs = list(outs)
    marks = [((8, 128), jnp.int32)]

    return pl.pallas_call(
        run,
        in_specs=[smem] * len(scalars) + [vmem] * (len(ins) + len(after)) + [held] * len(behind),
        out_specs=[vmem] * (len(outs) + 1),
        out_shape=[jax.ShapeDtypeStruct(shape, dtype) for shape, dtype in outs + marks],
        scratch_shapes=scratch,
        compiler_params=pltpu.CompilerParams(vmem_limit_bytes=16 * 1024 * 1024),
        cost_estimate=pl.CostEstimate(flops=flops, bytes_accessed=1024, transcendentals=0),
        name=name,
    )(*scalars, *ins, *after, *behind)


def relayout(kernel):
    rows, outer, inner = kernel.shape
    part = 512

    def body(in_ref, out_ref, mark_ref, wide_ref):
        mark_ref[...] = jnp.zeros_like(mark_ref)
        wide_ref[...] = in_ref[...].astype(jnp.float32).reshape(wide_ref.shape)
        span = pl.ds(pl.multiple_of(pl.program_id(0) * part, part), part)
        for r in range(outer):
            piece = wide_ref[pl.ds(r, part, stride=outer), :]
            out_ref[span, pl.ds(r * inner, inner)] = piece.astype(out_ref.dtype)

    vmem = pl.BlockSpec(memory_space=pltpu.VMEM)
    return pl.pallas_call(
        body,
        grid=(rows // part,),
        in_specs=[pl.BlockSpec((part, outer, inner), lambda i: (i, 0, 0))],
        out_specs=[vmem, vmem],
        out_shape=[
            jax.ShapeDtypeStruct((rows, outer * inner), kernel.dtype),
            jax.ShapeDtypeStruct((8, 128), jnp.int32),
        ],
        scratch_shapes=[pltpu.VMEM((part * outer, inner), jnp.float32)],
        compiler_params=pltpu.CompilerParams(vmem_limit_bytes=16 * 1024 * 1024),
        cost_estimate=pl.CostEstimate(flops=0, bytes_accessed=1024, transcendentals=0),
        name="relayout",
    )(kernel)


def terms(groups, order, first_block, panels, tile, outs, after=()):
    width = panels[0].shape[1]
    depth = panels[0].shape[0]
    cols = depth * len(panels)
    slots = tile.shape[1]
    sizes = [g.shape[0] for g in groups]
    col_part, out_part = 256, 768
    n_groups, n_panels = len(groups), len(panels)

    def body(order_ref, *refs):
        ins, refs = refs[:n_groups], refs[n_groups:]
        panel_refs, refs = refs[:n_panels], refs[n_panels:]
        tile_ref, refs = refs[0], refs[1:]
        out_refs, (weighted,) = refs[: len(outs)], refs[len(outs) :]
        for k in range(cols // col_part):
            panel_ref = panel_refs[k * col_part // depth]
            top = 0
            for ref, size in zip(ins, sizes):
                gram = lax.dot_general(
                    ref[...],
                    panel_ref[pl.ds(k * col_part % depth, col_part), :],
                    (((1,), (1,)), ((), ())),
                    preferred_element_type=jnp.float32,
                )
                for j in range(size // slots):
                    span = pl.ds(k * col_part, col_part)
                    part = gram[j * slots : (j + 1) * slots, :]
                    kern = tile_ref[order_ref[first_block + top // slots + j], :, span].astype(jnp.float32)
                    weighted[pl.ds(top + j * slots, slots), span] = (part * kern).astype(
                        jnp.bfloat16
                    )
                top += size
        for start in range(0, width, out_part):
            span = pl.ds(start, min(out_part, width - start))
            term = None
            for i, panel_ref in enumerate(panel_refs):
                more = jnp.dot(
                    weighted[:, pl.ds(i * depth, depth)],
                    panel_ref[:, span],
                    preferred_element_type=jnp.float32,
                )
                term = more if term is None else term + more
            for ref, (dtype, parts) in zip(out_refs, outs):
                at = 0
                for block, start, size in parts:
                    top = block * slots + start
                    ref[pl.ds(at, size), span] = term[top : top + size, :].astype(dtype)
                    at += size

    return whole_arrays(
        body,
        (*groups, *panels, tile),
        [((sum(p[2] for p in parts), width), dtype) for dtype, parts in outs],
        after=after,
        scalars=(order,),
        scratch=[pltpu.VMEM((sum(sizes), cols), jnp.bfloat16)],
        flops=4 * sum(sizes) * cols * width,
        name="terms",
    )


def stacks(pieces, after=(), behind=()):
    ins = [a for parts in pieces for a in parts]
    rows = [sum(a.shape[0] for a in parts) for parts in pieces]

    def body(*refs):
        i = 0
        for out, parts in zip(refs[len(ins) :], pieces):
            top = 0
            for a in parts:
                out[pl.ds(top, a.shape[0]), :] = refs[i][...]
                top += a.shape[0]
                i += 1

    outs = [((n, ins[0].shape[1]), ins[0].dtype) for n in rows]
    return whole_arrays(body, ins, outs, after=after, behind=behind, name="stacks")


def place(ins, order, first_place, slots, after=(), behind=()):
    rows, width = sum(a.shape[0] for a in ins), ins[0].shape[1]

    def body(order_ref, *refs):
        i = 0
        for ref, a in zip(refs, ins):
            for start in range(0, a.shape[0], slots):
                at = pl.multiple_of(order_ref[first_place + i] * slots, slots)
                refs[len(ins)][pl.ds(at, slots), :] = ref[pl.ds(start, slots), :]
                i += 1

    outs = [((rows, width), ins[0].dtype)]
    return whole_arrays(body, ins, outs, after=after, behind=behind, scalars=(order,), name="place")


def sums(mine, got, cuts, dtype, after=(), behind=()):
    rows, width = mine.shape
    size = rows // cuts

    def body(*refs):
        ins, outs = refs[: 1 + len(got)], refs[1 + len(got) :]
        for k, out in enumerate(outs):
            span = pl.ds(k * size, size)
            total = ins[0][span, :].astype(jnp.float32)
            for ref in ins[1:]:
                total = total + ref[span, :].astype(jnp.float32)
            out[...] = total.astype(dtype)

    outs = [((size, width), dtype)] * cuts
    return whole_arrays(body, (mine, *got), outs, after=after, behind=behind, name="sums")


def plane_perm(n_row, n_col, first, second):
    pairs = []
    for r in range(n_row):
        dx, dy = (first, second) if r % 2 == 0 else (second, first)
        for c in range(n_col):
            y, x = c // SIDE, c % SIDE
            to = ((y + dy) % SIDE) * SIDE + (x + dx) % SIDE
            pairs.append((r * n_col + c, r * n_col + to))
    return pairs


def solution(mesh):
    n_row, n_col = mesh.shape["row"], mesh.shape["col"]
    bf, f32 = jnp.bfloat16, jnp.float32

    def first(a, by):
        return lax.ppermute(a, ("row", "col"), plane_perm(n_row, n_col, by, 0))

    def second(a, by):
        return lax.ppermute(a, ("row", "col"), plane_perm(n_row, n_col, 0, by))

    def other_core(a):
        return lax.ppermute(a, "row", [(r, r ^ 1) for r in range(n_row)])

    def around_z(a):
        to = [(r + 2 - 4 * (r % 2)) % n_row for r in range(n_row)]
        return lax.ppermute(a, "row", list(enumerate(to)))

    def on_device(orbitals, point_cell, point_count, kernel):
        slab, width = orbitals.shape
        slots = point_cell.shape[2]

        offsets, b_offsets = (2, 1, -1, 0), (0, -1, 1, 2)
        row, col = lax.axis_index("row"), lax.axis_index("col")
        z, core, y, x = row // 2, row % 2, col // SIDE, col % SIDE
        order = []
        for b in b_offsets:
            for a in offsets:
                dx, dy = jnp.where(core == 0, a, b), jnp.where(core == 0, b, a)
                order.append(((y + dy) % SIDE) * SIDE + (x + dx) % SIDE)
        for of in (core, 1 - core):
            order += [2 * ((z + (2 * of - 1) * step + SIDE) % SIDE) + of for step in range(SIDE)]
        order = jnp.stack(order).astype(jnp.int32)

        own = pick(orbitals, point_cell.reshape(1, slots), point_count, order)
        tile, mark = relayout(kernel.reshape(n_col * slots, n_row, slots))
        tile = tile.reshape(n_col, slots, -1)
        far = first(own, 2)
        low, high = first(own, 1), first(own, -1)
        along = [own]
        for _ in range(SIDE - 1):
            along.append(around_z(along[-1]))
        wide, near, mark = stacks(((far, high), (low, own)), after=(mark,))
        near_low, wide_high = second(near, 1), second(wide, -1)
        wide_low, near_high = second(wide, 1), second(near, -1)
        mine, mark = stacks((along,), after=(mark,), behind=(near_low, wide_high))
        panel, mark = place(
            (mine, other_core(mine)),
            order,
            SIDE * SIDE,
            slots,
            after=(mark,),
        )

        def terms_of(groups, bs, after=()):
            outs = [
                (f32 if a == 0 else bf, [(4 * i + k, 0, slots) for i in range(len(bs))])
                for k, a in enumerate(offsets)
            ]
            at = SIDE * b_offsets.index(bs[0])
            return terms(groups, order, at, (panel,), tile, outs, after=after)

        def over_first(t):
            return first(t[0], 2), first(t[1], 1), first(t[2], -1)

        def total(mine, got):
            return mine + sum(a.astype(f32) for a in got)

        *t_here, mark = terms_of((wide, near), (0,), after=(mark,))
        got_here = over_first(t_here)
        near_far, wide_far = second(near_low, 1), second(wide_high, -1)
        *t_near, mark = terms_of((wide_low, near_low, wide_high, near_high), (-1, 1), after=(mark,))
        here, mark = sums(t_here[3], got_here, 1, f32, after=(mark,))
        got_near = over_first(t_near)
        *t_far, mark = terms_of((wide_far, near_far), (2,), after=(mark,))
        got_far = over_first(t_far)
        to_low, to_high, mark = sums(t_near[3], got_near, 2, bf, after=(mark,))
        got = second(to_low, -1), second(to_high, 1)
        to_far, _ = sums(t_far[3], got_far, 1, bf, after=(mark,), behind=got)
        result = total(here, (*got, second(to_far, 2)))
        return result.reshape(1, 1, slots, width)

    in_specs = (
        P(("row", "col"), None),
        P("row", "col", None),
        P("row", "col"),
        P("row", None, None, None, "col", None),
    )
    out_specs = P("row", "col", None, None)
    return jax.shard_map(
        on_device, mesh=mesh, in_specs=in_specs, out_specs=out_specs, check_vma=False
    )
```
